256 devices in a mesh: chan: 32 (over z, y_lo, core), tm: 8 (over y_hi, x).
Axes of the slice: x: 4, y: 4 (y_hi: 2, y_lo: 2; y = y_hi * 2 + y_lo), z: 8, core: 2. Of those that a mesh axis runs over, the one named last changes fastest.
Arguments:
- record: float32 [16384, 16384], P('tm', 'chan'), may hold values from -6 to 6
- coefficients: float32 [128, 2, 32, 16384], P('tm', None, 'chan'), may hold values from -3 to 3
- band_start: int32 [1], replicated, may hold values from 1 to 97
- band_level: int32 [32], replicated, may hold values from 0 to 7
- levels: float32 [8], replicated, may hold values from 0.3 to 2
Outputs:
- updated: float32 [128, 2, 32, 16384], P('tm', None, 'chan')
- residual: float32 [16384, 16384], P('tm', 'chan')
The draws below stay inside these ranges and needn't reach their ends.
Inputs may be any that keep to these rules, and one draw needn't show every extreme that they name: The band's bins band_start to band_start + 31 lie at or below bin 256 / 2.
All inputs are finite; a program needn't handle non-finite values.
Results may differ from the reference program's by a relative error of at most 0.000082.
Values sent between devices are 32-bit elements; how exact they have to be, the bound alone decides.
A program may use at most 192 MiB of HBM per device.

```python
import math
import jax
import jax.numpy as jnp
from jax import lax

CH = 16384
FRAME = 256
NB = 32
LEVELS = 8
HOP = 128
FRAMES = 128
SAMPLES = 16384


def with_ends(drawn, rng, low, top_value):
    longest = drawn.shape.index(max(drawn.shape))
    spots = []
    for shift in (0, 1):
        where = [jax.random.randint(jax.random.fold_in(rng, axis), (), 0, length) for axis, length in enumerate(drawn.shape)]
        where[longest] = (where[longest] + shift) % drawn.shape[longest]
        spots.append(tuple(where))
    return drawn.at[spots[0]].set(low).at[spots[1]].set(top_value)


def shard_levels(rng, shape, cuts, least, top_value):
    factor_of, own = 1.0, jax.random.fold_in(rng, 6)
    for dim, shards_of in cuts:
        heights = jnp.exp(jax.random.uniform(jax.random.fold_in(own, dim), (shards_of,), jnp.float32, least / len(cuts), top_value / len(cuts)))
        factor_of = factor_of * jnp.repeat(heights, shape[dim] // shards_of).reshape([-1 if axis == dim else 1 for axis in range(len(shape))])
    return factor_of


def gaussian(stream_key, extent, scale, reach, shards=(), kind=jnp.bfloat16):
    loudness = shard_levels(stream_key, extent, shards, -0.22, 0.18) if shards else 1.0
    values = jax.random.normal(stream_key, extent, jnp.float32) * scale * loudness
    return jnp.minimum(jnp.maximum(values, -reach), reach).astype(kind)


def setup_inputs(seed: int = 0) -> dict:
    streams_of = jax.random.split(jax.random.key(seed), 6)
    record = gaussian(streams_of[0], (SAMPLES, CH), 1.0, 6.0, ((0, 8), (1, 32)), jnp.float32)
    coefficients = gaussian(streams_of[1], (FRAMES, 2, NB, CH), 0.5, 3.0, ((0, 8), (2, 32)), jnp.float32)
    band_start = jax.random.randint(streams_of[2], (1,), 1, FRAME // 2 + 2 - NB).astype(jnp.int32)
    band_level = with_ends(jax.random.randint(streams_of[3], (NB,), 0, LEVELS), jax.random.fold_in(streams_of[3], 1), 0, LEVELS - 1).astype(jnp.int32)
    levels = jnp.clip(jnp.exp(jax.random.uniform(streams_of[4], (LEVELS,), jnp.float32, math.log(0.3), math.log(2.0))), 0.3, 2.0)
    return {"record": record, "coefficients": coefficients, "band_start": band_start, "band_level": band_level, "levels": levels}


HIGH = lax.Precision.HIGHEST

def frame_table(band_start, frame_len, bin_count):
    sample_idx = lax.broadcasted_iota(jnp.int32, (frame_len, bin_count), 0)
    bin_index = lax.broadcasted_iota(jnp.int32, (frame_len, bin_count), 1) + band_start[0]
    phases = (sample_idx * bin_index % frame_len).astype(jnp.float32) * (2.0 * math.pi / frame_len)
    window = jnp.sin((sample_idx.astype(jnp.float32) + 0.5) * (math.pi / frame_len))
    factor = 1.0 / math.sqrt(frame_len)
    return jnp.stack([window * jnp.cos(phases) * factor, -window * jnp.sin(phases) * factor], axis=1)

def reference(record, coefficients, band_start, band_level, levels):
    table = frame_table(band_start, FRAME, NB).astype(record.dtype)
    spectrum = jnp.fft.ifft(lax.complex(coefficients[:, 0], coefficients[:, 1]), axis=-1, norm='ortho')
    spectra = jnp.stack([jnp.real(spectrum), jnp.imag(spectrum)], axis=1)
    block_len = min(CH, 1024)
    block_count = CH // block_len
    spectra_blocks = jnp.transpose(spectra.reshape(FRAMES, 2, NB, block_count, block_len), (3, 0, 1, 2, 4))
    record_blocks = jnp.transpose(record.reshape(SAMPLES, block_count, block_len), (1, 0, 2))

    def per_block(items):
        spectra_blk, record_blk = items
        frames_out = 2.0 * jnp.einsum('frbc,nrb->fnc', spectra_blk, table, precision=HIGH)
        head_half = frames_out[:, :HOP]
        tail_half = frames_out[:, HOP:]
        following = jnp.concatenate([head_half[1:], jnp.zeros_like(head_half[:1])], axis=0)
        estimate = tail_half + following
        rest = record_blk.reshape(FRAMES, HOP, block_len) - estimate
        extended = jnp.concatenate([jnp.zeros_like(rest[:1]), rest], axis=0)
        windows = jnp.concatenate([extended[:-1], extended[1:]], axis=1)
        analysed = jnp.einsum('fnc,nrb->frbc', windows, table, precision=HIGH)
        return (analysed, rest.reshape(SAMPLES, block_len))
    analysed, residual = lax.map(per_block, (spectra_blocks, record_blocks))
    analysed = jnp.transpose(analysed, (1, 2, 3, 0, 4)).reshape(FRAMES, 2, NB, CH)
    residual = jnp.transpose(residual, (1, 0, 2)).reshape(SAMPLES, CH)
    forward = jnp.fft.fft(lax.complex(analysed[:, 0], analysed[:, 1]), axis=-1, norm='ortho')
    combined = coefficients + jnp.stack([jnp.real(forward), jnp.imag(forward)], axis=1)
    limits = levels[band_level]
    magnitude = jnp.sqrt(combined[:, 0] * combined[:, 0] + combined[:, 1] * combined[:, 1])
    limit_b = limits[None, :, None]
    shrink = jnp.maximum(magnitude - limit_b, 0.0) / jnp.maximum(magnitude, limit_b)
    updated = combined * shrink[:, None]
    return (updated, residual)
```

```python
import functools
import math

import jax
import jax.numpy as jnp
import ml_dtypes
import numpy as np
from jax import lax
from jax.experimental import pallas as pl
from jax.experimental.pallas import tpu as pltpu
from jax.sharding import PartitionSpec as P

FRAME = 256
HOP = 128
NB = 32
CHUNK = 4
MESH = pl.DeviceIdType.MESH
F32 = jnp.float32
BF16 = jnp.bfloat16


def halves_of(table):
    high = table.astype(ml_dtypes.bfloat16)
    low = (table - high.astype(np.float64)).astype(ml_dtypes.bfloat16)
    return np.stack([high, low])


def dft_tables(devices):
    side = 128
    idx = np.arange(side)
    angle = 2.0 * math.pi * (np.outer(idx, idx) % side) / side
    c, s = np.cos(angle), np.sin(angle)
    inverse = np.block([[c, -s], [s, c]])
    per = side // devices
    order = [r * side + d * per + q for d in range(devices) for r in range(2) for q in range(per)]
    first = inverse
    second = inverse[order]
    turn = 2.0 * math.pi * np.outer(idx, idx) / side**2
    twist = np.stack([np.cos(turn), np.sin(turn)]).astype(np.float32) / np.float32(side)
    return halves_of(first), halves_of(second), halves_of(second.T), halves_of(first.T), twist


def window_table():
    n = np.arange(HOP)[:, None] + np.where(np.arange(4 * NB)[None] < 2 * NB, HOP, 0)
    return (np.sin((n + 0.5) * (math.pi / FRAME)) / math.sqrt(FRAME)).astype(np.float32)


def split(x):
    high = x.astype(BF16)
    return high, (x - high.astype(F32)).astype(BF16)


def dot3(matrix, x, transposed=False):
    high, low = split(x)
    dims = (((1,), (1 if transposed else 0,)), ((), ()))
    dot = functools.partial(lax.dot_general, dimension_numbers=dims, preferred_element_type=F32)
    return dot(matrix[0], high) + (dot(matrix[0], low) + dot(matrix[1], high))


def kernel(
    n_chan, n_tm,
    start_ref, level_ref, levels_ref, coef_hbm, rec_hbm, first_ref, second_ref, back1_ref, back2_ref, twist_ref, window_ref, windowt_ref,
    upd_hbm, res_hbm,
    coef, rec, send_f, recv_f, send_b, recv_b, halo_s, halo_p, send_p, carry, synth, analy,
    in_sem, out_sem, ssem_f, rsem_f, ssem_b, rsem_b, hsend, hrecv,
):
    me = lax.axis_index("chan")
    t = lax.axis_index("tm")
    before, after = lax.rem(t + n_tm - 1, n_tm), lax.rem(t + 1, n_tm)
    frames = coef.shape[0]
    chunks = frames // CHUNK
    side = 128

    load_coef = pltpu.make_async_copy(coef_hbm, coef, in_sem.at[0])
    load_rec = pltpu.make_async_copy(rec_hbm, rec, in_sem.at[1])
    load_coef.start()
    load_rec.start()

    barrier = pltpu.get_barrier_semaphore()

    def greet(i, _):
        pl.semaphore_signal(barrier, inc=1, device_id={"chan": lax.rem(me + i, n_chan)}, device_id_type=MESH)
        return 0

    lax.fori_loop(1, n_chan, greet, 0)
    for other in (before, after):
        pl.semaphore_signal(barrier, inc=1, device_id={"tm": other}, device_id_type=MESH)

    def forward(j):
        for pair in range(CHUNK // 2):
            q = j * CHUNK + 2 * pair
            lanes = [coef[lax.rem(q + a + frames - 1, frames)] for a in range(2)]
            y = dot3(first_ref, jnp.concatenate(lanes, axis=1))
            rows = []
            for a in range(2):
                yr, yi = y[:side, a * side:(a + 1) * side], y[side:, a * side:(a + 1) * side]
                tr = yr * twist_ref[0] - yi * twist_ref[1]
                ti = yr * twist_ref[1] + yi * twist_ref[0]
                rows.append(jnp.concatenate([tr, ti], axis=1))
            x = dot3(second_ref, jnp.concatenate(rows, axis=0), True)
            for a in range(2):
                send_f[j, 2 * pair + a] = x[:, a * side:(a + 1) * side]

    def exchange(src, dst, ssem, rsem, j):
        mine = pl.ds(pl.multiple_of(me * 8, 8), 8)

        def one(i, _):
            d = lax.rem(me + i, n_chan)
            pltpu.make_async_remote_copy(
                src_ref=src.at[j, :, pl.ds(pl.multiple_of(d * 8, 8), 8)],
                dst_ref=dst.at[j, :, mine],
                send_sem=ssem.at[j],
                recv_sem=rsem.at[j],
                device_id={"chan": d},
                device_id_type=MESH,
            ).start()
            return 0

        lax.fori_loop(1, n_chan, one, 0)
        pltpu.make_async_copy(src.at[j, :, mine], dst.at[j, :, mine], rsem.at[j]).start()

    def wait_bytes(ref, sem):
        pltpu.make_async_copy(ref, ref, sem).wait()

    load_coef.wait()
    forward(0)
    pl.semaphore_wait(barrier, n_chan + 1)
    exchange(send_f, recv_f, ssem_f, rsem_f, 0)

    def forward_step(j, _):
        forward(j)
        exchange(send_f, recv_f, ssem_f, rsem_f, j)
        return 0

    lax.fori_loop(1, chunks, forward_step, 0)

    start = start_ref[0]

    def wave(n_axis, window):
        n_idx = lax.broadcasted_iota(jnp.int32, (side, side), n_axis)
        col = lax.broadcasted_iota(jnp.int32, (side, side), 1 - n_axis)
        later = jnp.where(col < 2 * NB, HOP, 0)
        within = col & (2 * NB - 1)
        phase = ((n_idx + later) * (start + (within >> 1)) + (within & 1) * (FRAME // 4)) & (FRAME - 1)
        return window * jnp.cos(phase.astype(F32) * (2.0 * math.pi / FRAME))

    synth[0], synth[1] = split(2.0 * wave(0, window_ref[...]))
    analy[0], analy[1] = split(wave(1, windowt_ref[...]))
    carry[...] = jnp.zeros_like(carry)
    load_rec.wait()

    def spectra(i, tile):
        q = lax.rem(i + 1, frames)
        return recv_f[q // CHUNK, lax.rem(q, CHUNK), pl.ds(tile, 2 * NB, stride=4)]

    def residual_half(i, h, own, following):
        cols = slice(h * 256, (h + 1) * 256)
        est = dot3(synth, jnp.concatenate([jnp.concatenate(own, axis=1), jnp.concatenate(following, axis=1)], axis=0))
        rest = rec[i, :, cols] - est
        rec[i, :, cols] = rest
        return dot3(analy, rest)

    def put(i, tile, value, add=False):
        p = lax.rem(i + frames - 2, frames)
        where = (p // CHUNK, lax.rem(p, CHUNK), pl.ds(tile, 2 * NB, stride=4))
        send_b[where] = value + send_b[where] if add else value

    def store_residual(i):
        pltpu.make_async_copy(rec.at[i], res_hbm.at[i], out_sem.at[0]).start()

    def step(i, _):
        for h in range(2):
            cols = slice(h * 256, (h + 1) * 256)
            tiles = (2 * h, 2 * h + 1)
            part = residual_half(i, h, [spectra(i, k) for k in tiles], [spectra(i + 1, k) for k in tiles])
            analysed = part[:2 * NB] + carry[:, cols]
            carry[:, cols] = part[2 * NB:]
            for a, k in enumerate(tiles):
                put(i, k, analysed[:, a * side:(a + 1) * side])
        store_residual(i)
        return 0

    wait_bytes(recv_f.at[0], rsem_f.at[0])
    halo_out = pltpu.make_async_remote_copy(
        src_ref=recv_f.at[0, 1], dst_ref=halo_s, send_sem=hsend.at[0], recv_sem=hrecv.at[0],
        device_id={"tm": before}, device_id_type=MESH)
    halo_out.start()
    lax.fori_loop(0, CHUNK - 2, step, 0)

    def middle(j):
        wait_bytes(recv_f.at[j], rsem_f.at[j])
        lax.fori_loop(j * CHUNK - 2, j * CHUNK + 2, step, 0)
        exchange(send_b, recv_b, ssem_b, rsem_b, j - 1)

    middle(1)

    halo_out.wait()
    last = frames - 1
    for h in range(2):
        tiles = (2 * h, 2 * h + 1)
        following = [jnp.where(t < n_tm - 1, halo_s[pl.ds(k, 2 * NB, stride=4)], 0.0) for k in tiles]
        part = residual_half(last, h, [spectra(last, k) for k in tiles], following)
        send_p[:, h * 256:(h + 1) * 256] = part[2 * NB:]
        for a, k in enumerate(tiles):
            put(last, k, part[:2 * NB, a * side:(a + 1) * side])
    store_residual(last)
    part_out = pltpu.make_async_remote_copy(
        src_ref=send_p, dst_ref=halo_p, send_sem=hsend.at[1], recv_sem=hrecv.at[1],
        device_id={"tm": after}, device_id_type=MESH)
    part_out.start()

    def middle_step(j, _):
        middle(j)
        return 0

    lax.fori_loop(2, chunks, middle_step, 0)
    step(frames - 2, 0)
    part_out.wait()
    for k in range(4):
        cols = slice(k * side, (k + 1) * side)
        put(last, k, carry[:, cols], True)
        put(0, k, jnp.where(t > 0, halo_p[:, cols], 0.0), True)
    exchange(send_b, recv_b, ssem_b, rsem_b, chunks - 1)

    limit = levels_ref[level_ref[me]]

    def backward(j, _):
        wait_bytes(recv_b.at[j], rsem_b.at[j])
        for pair in range(CHUNK // 2):
            y = dot3(back1_ref, jnp.concatenate([recv_b[j, 2 * pair], recv_b[j, 2 * pair + 1]], axis=1))
            rows = []
            for a in range(2):
                yr, yi = y[:side, a * side:(a + 1) * side], y[side:, a * side:(a + 1) * side]
                tr = yr * twist_ref[0] + yi * twist_ref[1]
                ti = yi * twist_ref[0] - yr * twist_ref[1]
                rows.append(jnp.concatenate([tr, ti], axis=1))
            u = dot3(back2_ref, jnp.concatenate(rows, axis=0), True)
            for a in range(2):
                f = lax.rem(j * CHUNK + 2 * pair + a + 2, frames)
                cr = coef[f, :side] + u[:side, a * side:(a + 1) * side]
                ci = coef[f, side:] + u[side:, a * side:(a + 1) * side]
                m = jnp.sqrt(cr * cr + ci * ci)
                shrink = jnp.maximum(m - limit, 0.0) / jnp.maximum(m, limit)
                coef[f, :side] = cr * shrink
                coef[f, side:] = ci * shrink
                pltpu.make_async_copy(coef.at[f], upd_hbm.at[f], out_sem.at[1]).start()
        return 0

    lax.fori_loop(0, chunks, backward, 0)

    def drain(j, _):
        for buf, sem in ((send_f, ssem_f), (send_b, ssem_b)):
            wait_bytes(buf.at[j, :, pl.ds(0, 8 * (n_chan - 1))], sem.at[j])
        return 0

    lax.fori_loop(0, chunks, drain, 0)
    wait_bytes(rec, out_sem.at[0])
    wait_bytes(coef, out_sem.at[1])


def body(n_chan, n_tm, record, coefficients, band_start, band_level, levels):
    rows, cols = record.shape
    frames = coefficients.shape[0]
    chunks = frames // CHUNK
    window = window_table()
    tables = [jnp.asarray(x) for x in (*dft_tables(n_chan), window, window.T.copy())]
    vmem, smem, hbm = (pl.BlockSpec(memory_space=m) for m in (pltpu.VMEM, pltpu.SMEM, pl.ANY))
    block = pltpu.VMEM((chunks, CHUNK, 8 * n_chan, 128), F32)
    updated, residual = pl.pallas_call(
        functools.partial(kernel, n_chan, n_tm),
        out_shape=(jax.ShapeDtypeStruct((frames, 256, 128), F32), jax.ShapeDtypeStruct((frames, HOP, cols), F32)),
        in_specs=[smem] * 3 + [hbm] * 2 + [vmem] * len(tables),
        out_specs=(hbm, hbm),
        scratch_shapes=[
            pltpu.VMEM((frames, 256, 128), F32),
            pltpu.VMEM((frames, HOP, cols), F32),
            block, block, block, block,
            pltpu.VMEM((8 * n_chan, 128), F32),
            pltpu.VMEM((2 * NB, cols), F32),
            pltpu.VMEM((2 * NB, cols), F32),
            pltpu.VMEM((2 * NB, cols), F32),
            pltpu.VMEM((2, 128, 128), BF16),
            pltpu.VMEM((2, 128, 128), BF16),
            pltpu.SemaphoreType.DMA((2,)),
            pltpu.SemaphoreType.DMA((2,)),
            pltpu.SemaphoreType.DMA((chunks,)),
            pltpu.SemaphoreType.DMA((chunks,)),
            pltpu.SemaphoreType.DMA((chunks,)),
            pltpu.SemaphoreType.DMA((chunks,)),
            pltpu.SemaphoreType.DMA((2,)),
            pltpu.SemaphoreType.DMA((2,)),
        ],
        compiler_params=pltpu.CompilerParams(
            collective_id=0, has_side_effects=True, vmem_limit_bytes=48 * 1024 * 1024
        ),
    )(
        band_start, band_level, levels,
        coefficients.reshape(frames, 256, 128), record.reshape(frames, HOP, cols), *tables,
    )
    return updated.reshape(coefficients.shape), residual.reshape(rows, cols)


def solution(mesh):
    return jax.shard_map(
        functools.partial(body, mesh.shape["chan"], mesh.shape["tm"]),
        mesh=mesh,
        in_specs=(P("tm", "chan"), P("tm", None, "chan", None), P(), P(), P()),
        out_specs=(P("tm", None, "chan", None), P("tm", "chan")),
        check_vma=False,
    )
```

```python
import functools
import math

import jax
import jax.numpy as jnp
import numpy as np
from jax import lax
from jax.experimental import pallas as pl
from jax.experimental.pallas import tpu as pltpu
from jax.sharding import PartitionSpec as P

FRAME = 256
HOP = 128
NB = 32
CHUNK = 4
VMEM_LIMIT = 60 * 1024 * 1024
PIECES = 8
MESH = pl.DeviceIdType.MESH
F32 = jnp.float32
BF16 = jnp.bfloat16


def dft_tables(devices):
    side = 128
    idx = np.arange(side)
    angle = 2.0 * math.pi * (np.outer(idx, idx) % side) / side
    c, s = np.cos(angle), np.sin(angle)
    inverse = np.block([[c, -s], [s, c]])
    per = side // devices
    order = [r * side + d * per + q for d in range(devices) for r in range(2) for q in range(per)]
    second = inverse[order]
    turn = 2.0 * math.pi * np.outer(idx, idx) / side**2
    twist = np.stack([np.cos(turn), np.sin(turn)]).astype(np.float32) / np.float32(side)
    return np.stack([inverse, second, second.T, inverse.T]).astype(np.float32), twist


def window_table():
    n = np.arange(HOP)[:, None] + np.where(np.arange(4 * NB)[None] < 2 * NB, HOP, 0)
    return (np.sin((n + 0.5) * (math.pi / FRAME)) / math.sqrt(FRAME)).astype(np.float32)


def split(x):
    high = x.astype(BF16)
    return high, (x - high.astype(F32)).astype(BF16)


def dot3(matrix, x, transposed=False):
    high, low = split(x)
    dims = (((1,), (1 if transposed else 0,)), ((), ()))
    dot = functools.partial(lax.dot_general, dimension_numbers=dims, preferred_element_type=F32)
    return dot(matrix[0], high) + (dot(matrix[0], low) + dot(matrix[1], high))


def two_steps(matrices, k, twist, conj, pair):
    side = 128
    y = dot3(matrices.at[k], jnp.concatenate(pair, axis=1))
    rows = []
    for a in range(2):
        yr, yi = y[:side, a * side:(a + 1) * side], y[side:, a * side:(a + 1) * side]
        if conj:
            tr, ti = yr * twist[0] + yi * twist[1], yi * twist[0] - yr * twist[1]
        else:
            tr, ti = yr * twist[0] - yi * twist[1], yr * twist[1] + yi * twist[0]
        rows.append(jnp.concatenate([tr, ti], axis=1))
    return dot3(matrices.at[k + 1], jnp.concatenate(rows, axis=0), True)


def shrunk(coef, u, limit):
    cr, ci = coef[:128] + u[:128], coef[128:] + u[128:]
    m = jnp.sqrt(cr * cr + ci * ci)
    factor = jnp.maximum(m - limit, 0.0) / jnp.maximum(m, limit)
    return cr * factor, ci * factor


def kernel(
    n_chan, n_tm,
    start_hbm, level_hbm, levels_hbm, coef_hbm, rec_hbm, tables_hbm, twist_hbm, window_hbm,
    upd_hbm, res_hbm, last_hbm,
    coef, rec, send_f, recv_f, send_b, recv_b, halo_s, halo_p, send_p, carry, synth, analy, tables, ahead, back, twist, window,
    start_ref, level_ref, levels_ref,
    in_sem, out_sem, ssem_f, rsem_f, ssem_b, rsem_b, hsend, hrecv,
):
    me = lax.axis_index("chan")
    t = lax.axis_index("tm")
    before, after = lax.rem(t + n_tm - 1, n_tm), lax.rem(t + 1, n_tm)
    frames = coef.shape[0]
    chunks = frames // CHUNK
    side = 128

    early = [(tables_hbm, tables), (twist_hbm, twist),
             (coef_hbm.at[frames - 1], coef.at[frames - 1]),
             (coef_hbm.at[pl.ds(0, CHUNK - 1)], coef.at[pl.ds(0, CHUNK - 1)])]
    later = [(coef_hbm.at[pl.ds(CHUNK - 1, frames - CHUNK)], coef.at[pl.ds(CHUNK - 1, frames - CHUNK)]),
             (window_hbm, window), (start_hbm, start_ref), (level_hbm, level_ref), (levels_hbm, levels_ref),
             (rec_hbm, rec)]
    loads = [pltpu.make_async_copy(src, dst, in_sem.at[i]) for i, (src, dst) in enumerate(early + later)]

    barrier = pltpu.get_barrier_semaphore()

    def greet(i, _):
        pl.semaphore_signal(barrier, inc=1, device_id={"chan": lax.rem(me + i, n_chan)}, device_id_type=MESH)
        return 0

    lax.fori_loop(1, n_chan, greet, 0)
    for other in (before, after):
        pl.semaphore_signal(barrier, inc=1, device_id={"tm": other}, device_id_type=MESH)
    for load in loads:
        load.start()

    def forward(j):
        for pair in range(CHUNK // 2):
            q = j * CHUNK + 2 * pair
            x = two_steps(ahead, 0, twist, False, [coef[lax.rem(q + a + frames - 1, frames)] for a in range(2)])
            for a in range(2):
                send_f[j, 2 * pair + a] = x[:, a * side:(a + 1) * side]

    def exchange(src, dst, ssem, rsem, j):
        mine = pl.ds(pl.multiple_of(me * 8, 8), 8)

        def one(i, _):
            d = lax.rem(me + i, n_chan)
            pltpu.make_async_remote_copy(
                src_ref=src.at[j, :, pl.ds(pl.multiple_of(d * 8, 8), 8)],
                dst_ref=dst.at[j, :, mine],
                send_sem=ssem.at[j],
                recv_sem=rsem.at[j],
                device_id={"chan": d},
                device_id_type=MESH,
            ).start()
            return 0

        lax.fori_loop(1, n_chan, one, 0)
        pltpu.make_async_copy(src.at[j, :, mine], dst.at[j, :, mine], rsem.at[j]).start()

    def wait_bytes(ref, sem):
        pltpu.make_async_copy(ref, ref, sem).wait()

    for load in loads[:len(early)]:
        load.wait()
    for k in range(2):
        ahead[k, 0], ahead[k, 1] = split(tables[k])
    forward(0)
    pl.semaphore_wait(barrier, n_chan + 1)
    exchange(send_f, recv_f, ssem_f, rsem_f, 0)

    def forward_step(j, _):
        forward(j)
        exchange(send_f, recv_f, ssem_f, rsem_f, j)
        return 0

    for load in loads[len(early):-1]:
        load.wait()
    lax.fori_loop(1, chunks, forward_step, 0)

    start = start_ref[0]

    def wave(n_axis, window):
        n_idx = lax.broadcasted_iota(jnp.int32, (side, side), n_axis)
        col = lax.broadcasted_iota(jnp.int32, (side, side), 1 - n_axis)
        later = jnp.where(col < 2 * NB, HOP, 0)
        within = col & (2 * NB - 1)
        phase = ((n_idx + later) * (start + (within >> 1)) + (within & 1) * (FRAME // 4)) & (FRAME - 1)
        return window * jnp.cos(phase.astype(F32) * (2.0 * math.pi / FRAME))

    synth[0], synth[1] = split(2.0 * wave(0, window[0]))
    analy[0], analy[1] = split(wave(1, window[1]))
    carry[...] = jnp.zeros_like(carry)
    limit = levels_ref[level_ref[me]]
    for k in range(2):
        back[k, 0], back[k, 1] = split(tables[2 + k])
    loads[-1].wait()

    def spectra(i, tile):
        q = lax.rem(i + 1, frames)
        return recv_f[q // CHUNK, lax.rem(q, CHUNK), pl.ds(tile, 2 * NB, stride=4)]

    def residual_half(i, h, own, following):
        cols = slice(h * 256, (h + 1) * 256)
        est = dot3(synth, jnp.concatenate([jnp.concatenate(own, axis=1), jnp.concatenate(following, axis=1)], axis=0))
        rest = rec[i, :, cols] - est
        rec[i, :, cols] = rest
        return dot3(analy, rest)

    def store_residual(i):
        pltpu.make_async_copy(rec.at[i], res_hbm.at[i], out_sem.at[0]).start()

    def put(i, tile, value, add=False):
        p = lax.rem(i + frames - 2, frames)
        where = (p // CHUNK, lax.rem(p, CHUNK), pl.ds(tile, 2 * NB, stride=4))
        send_b[where] = value + send_b[where] if add else value

    def step(i, _):
        for h in range(2):
            cols = slice(h * 256, (h + 1) * 256)
            tiles = (2 * h, 2 * h + 1)
            part = residual_half(i, h, [spectra(i, k) for k in tiles], [spectra(i + 1, k) for k in tiles])
            analysed = part[:2 * NB] + carry[:, cols]
            carry[:, cols] = part[2 * NB:]
            for a, k in enumerate(tiles):
                put(i, k, analysed[:, a * side:(a + 1) * side])
        store_residual(i)
        return 0

    wait_bytes(recv_f.at[0], rsem_f.at[0])
    halo_out = pltpu.make_async_remote_copy(
        src_ref=recv_f.at[0, 1], dst_ref=halo_s, send_sem=hsend.at[0], recv_sem=hrecv.at[0],
        device_id={"tm": before}, device_id_type=MESH)
    halo_out.start()
    lax.fori_loop(0, CHUNK - 2, step, 0)

    def middle(j):
        wait_bytes(recv_f.at[j], rsem_f.at[j])
        lax.fori_loop(j * CHUNK - 2, j * CHUNK + 2, step, 0)
        exchange(send_b, recv_b, ssem_b, rsem_b, j - 1)

    middle(1)

    halo_out.wait()
    last = frames - 1
    for h in range(2):
        tiles = (2 * h, 2 * h + 1)
        following = [jnp.where(t < n_tm - 1, halo_s[pl.ds(k, 2 * NB, stride=4)], 0.0) for k in tiles]
        part = residual_half(last, h, [spectra(last, k) for k in tiles], following)
        send_p[:, h * 256:(h + 1) * 256] = part[2 * NB:]
        for a, k in enumerate(tiles):
            put(last, k, part[:2 * NB, a * side:(a + 1) * side])
    store_residual(last)
    part_out = pltpu.make_async_remote_copy(
        src_ref=send_p, dst_ref=halo_p, send_sem=hsend.at[1], recv_sem=hrecv.at[1],
        device_id={"tm": after}, device_id_type=MESH)
    part_out.start()

    def middle_step(j, _):
        middle(j)
        return 0

    lax.fori_loop(2, chunks, middle_step, 0)
    step(frames - 2, 0)
    part_out.wait()
    for k in range(4):
        cols = slice(k * side, (k + 1) * side)
        put(last, k, carry[:, cols], True)
        put(0, k, jnp.where(t > 0, halo_p[:, cols], 0.0), True)
    exchange(send_b, recv_b, ssem_b, rsem_b, chunks - 1)

    def backward(j, _):
        wait_bytes(recv_b.at[j], rsem_b.at[j])
        for pair in range(CHUNK // 2):
            u = two_steps(back, 0, twist, True, [recv_b[j, 2 * pair], recv_b[j, 2 * pair + 1]])
            for a in range(2):
                f = lax.rem(j * CHUNK + 2 * pair + a + 2, frames)
                coef[f, :side], coef[f, side:] = shrunk(coef[f], u[:, a * side:(a + 1) * side], limit)
        done = pl.ds(j * CHUNK + 2, CHUNK)
        pltpu.make_async_copy(coef.at[done], upd_hbm.at[done], out_sem.at[1]).start()
        return 0

    lax.fori_loop(0, chunks - 1, backward, 0)

    def drain(j, _):
        for buf, sem in ((send_f, ssem_f), (send_b, ssem_b)):
            wait_bytes(buf.at[j, :, pl.ds(0, 8 * (n_chan - 1))], sem.at[j])
        return 0

    lax.fori_loop(0, chunks, drain, 0)
    wait_bytes(rec, out_sem.at[0])
    wait_bytes(coef.at[pl.ds(0, frames - CHUNK)], out_sem.at[1])
    wait_bytes(recv_b.at[chunks - 1], rsem_b.at[chunks - 1])
    give = pltpu.make_async_copy(recv_b.at[chunks - 1], last_hbm, out_sem.at[2])
    give.start()
    give.wait()


def finish(
    level_hbm, levels_hbm, coef_hbm, tables_hbm, twist_hbm, last_hbm, upd1_hbm, res1_hbm,
    upd_hbm, res_hbm,
    last_b, coef, upd, rec, tables, back, twist, level_ref, levels_ref, in_sem, move_sem, out_sem,
):
    frames = coef_hbm.shape[0]
    loads = [pltpu.make_async_copy(src, dst, in_sem.at[i]) for i, (src, dst) in enumerate([
        (last_hbm, last_b), (tables_hbm.at[pl.ds(2, 2)], tables), (twist_hbm, twist),
        (coef_hbm.at[pl.ds(frames - 2, 2)], coef.at[0]), (coef_hbm.at[pl.ds(0, 2)], coef.at[1]),
        (level_hbm, level_ref), (levels_hbm, levels_ref)])]
    moves, stores = [], []
    spans = [(upd1_hbm, upd, upd_hbm, 2, frames - CHUNK)]
    spans += [(res1_hbm, rec, res_hbm, i * frames // PIECES, frames // PIECES) for i in range(PIECES)]
    for i, (src, via, dst, at, size) in enumerate(spans):
        some = pl.ds(at, size)
        moves.append((pltpu.make_async_copy(src.at[some], via.at[some], move_sem.at[i]),
                      pltpu.make_async_copy(via.at[some], dst.at[some], out_sem.at[i])))
    for load in loads:
        load.start()
    for load, _ in moves:
        load.start()
    for load in loads:
        load.wait()
    for k in range(2):
        back[k, 0], back[k, 1] = split(tables[k])

    def forward_moves(some):
        for load, store in some:
            load.wait()
            store.start()
            stores.append(store)

    limit = levels_ref[level_ref[lax.axis_index("chan")]]
    forward_moves(moves[:2])
    for pair in range(CHUNK // 2):
        u = two_steps(back, 0, twist, True, [last_b[2 * pair], last_b[2 * pair + 1]])
        for a in range(2):
            coef[pair, a, :128], coef[pair, a, 128:] = shrunk(coef[pair, a], u[:, a * 128:(a + 1) * 128], limit)
        first = (frames - CHUNK + 2 * pair + 2) % frames
        store = pltpu.make_async_copy(coef.at[pair], upd_hbm.at[pl.ds(first, 2)], out_sem.at[len(moves) + pair])
        store.start()
        stores.append(store)
        if pair == 0:
            forward_moves(moves[2:])
    for store in stores:
        store.wait()


def body(n_chan, n_tm, record, coefficients, band_start, band_level, levels):
    rows, cols = record.shape
    frames = coefficients.shape[0]
    chunks = frames // CHUNK
    window = window_table()
    tables, twist = dft_tables(n_chan)
    constants = [jnp.asarray(x) for x in (tables, twist, np.stack([window, window.T]))]
    hbm = pl.BlockSpec(memory_space=pl.ANY)
    block = pltpu.VMEM((chunks, CHUNK, 8 * n_chan, 128), F32)
    coef_shape = jax.ShapeDtypeStruct((frames, 256, 128), F32)
    rec_shape = jax.ShapeDtypeStruct((frames, HOP, cols), F32)
    coef_in, rec_in = coefficients.reshape(frames, 256, 128), record.reshape(frames, HOP, cols)
    upd1, res1, last_b = pl.pallas_call(
        functools.partial(kernel, n_chan, n_tm),
        out_shape=(
            coef_shape,
            rec_shape,
            jax.ShapeDtypeStruct((CHUNK, 8 * n_chan, 128), F32),
        ),
        in_specs=[hbm] * 8,
        out_specs=(hbm,) * 3,
        scratch_shapes=[
            pltpu.VMEM((frames, 256, 128), F32),
            pltpu.VMEM((frames, HOP, cols), F32),
            block, block, block, block,
            pltpu.VMEM((8 * n_chan, 128), F32),
            pltpu.VMEM((2 * NB, cols), F32),
            pltpu.VMEM((2 * NB, cols), F32),
            pltpu.VMEM((2 * NB, cols), F32),
            pltpu.VMEM((2, 128, 128), BF16),
            pltpu.VMEM((2, 128, 128), BF16),
            pltpu.VMEM((4, 256, 256), F32),
            pltpu.VMEM((2, 2, 256, 256), BF16),
            pltpu.VMEM((2, 2, 256, 256), BF16),
            pltpu.VMEM((2, 128, 128), F32),
            pltpu.VMEM((2, 128, 128), F32),
            pltpu.SMEM(band_start.shape, jnp.int32),
            pltpu.SMEM(band_level.shape, jnp.int32),
            pltpu.SMEM(levels.shape, F32),
            pltpu.SemaphoreType.DMA((10,)),
            pltpu.SemaphoreType.DMA((3,)),
            pltpu.SemaphoreType.DMA((chunks,)),
            pltpu.SemaphoreType.DMA((chunks,)),
            pltpu.SemaphoreType.DMA((chunks,)),
            pltpu.SemaphoreType.DMA((chunks,)),
            pltpu.SemaphoreType.DMA((2,)),
            pltpu.SemaphoreType.DMA((2,)),
        ],
        compiler_params=pltpu.CompilerParams(
            collective_id=0, has_side_effects=True, vmem_limit_bytes=VMEM_LIMIT
        ),
    )(
        band_start, band_level, levels, coef_in, rec_in, *constants,
    )
    updated, residual = pl.pallas_call(
        finish,
        out_shape=(coef_shape, rec_shape),
        in_specs=[hbm] * 8,
        out_specs=(hbm, hbm),
        scratch_shapes=[
            pltpu.VMEM((CHUNK, 8 * n_chan, 128), F32),
            pltpu.VMEM((CHUNK // 2, 2, 256, 128), F32),
            pltpu.VMEM((frames, 256, 128), F32),
            pltpu.VMEM((frames, HOP, cols), F32),
            pltpu.VMEM((2, 256, 256), F32),
            pltpu.VMEM((2, 2, 256, 256), BF16),
            pltpu.VMEM((2, 128, 128), F32),
            pltpu.SMEM(band_level.shape, jnp.int32),
            pltpu.SMEM(levels.shape, F32),
            pltpu.SemaphoreType.DMA((7,)),
            pltpu.SemaphoreType.DMA((PIECES + 1,)),
            pltpu.SemaphoreType.DMA((PIECES + 1 + CHUNK // 2,)),
        ],
        compiler_params=pltpu.CompilerParams(vmem_limit_bytes=VMEM_LIMIT),
    )(band_level, levels, coef_in, constants[0], constants[1], last_b, upd1, res1)
    return updated.reshape(coefficients.shape), residual.reshape(rows, cols)


def solution(mesh):
    return jax.shard_map(
        functools.partial(body, mesh.shape["chan"], mesh.shape["tm"]),
        mesh=mesh,
        in_specs=(P("tm", "chan"), P("tm", None, "chan", None), P(), P(), P()),
        out_specs=(P("tm", None, "chan", None), P("tm", "chan")),
        check_vma=False,
    )
```

```python
import functools
import math

import jax
import jax.numpy as jnp
import numpy as np
from jax import lax
from jax.experimental import pallas as pl
from jax.experimental.pallas import tpu as pltpu
from jax.sharding import PartitionSpec as P

FRAME = 256
HOP = 128
NB = 32
CHUNK = 4
VMEM_LIMIT = 40 * 1024 * 1024
MESH = pl.DeviceIdType.MESH
F32 = jnp.float32
BF16 = jnp.bfloat16


def dft_tables(devices):
    side = 128
    idx = np.arange(side)
    angle = 2.0 * math.pi * (np.outer(idx, idx) % side) / side
    c, s = np.cos(angle), np.sin(angle)
    inverse = np.block([[c, -s], [s, c]])
    per = side // devices
    order = [r * side + d * per + q for d in range(devices) for r in range(2) for q in range(per)]
    second = inverse[order]
    turn = 2.0 * math.pi * np.outer(idx, idx) / side**2
    twist = np.stack([np.cos(turn), np.sin(turn)]).astype(np.float32) / np.float32(side)
    return np.stack([inverse, second, second.T, inverse.T]).astype(np.float32), twist


def window_table():
    n = np.arange(HOP)[:, None] + np.where(np.arange(4 * NB)[None] < 2 * NB, HOP, 0)
    return (np.sin((n + 0.5) * (math.pi / FRAME)) / math.sqrt(FRAME)).astype(np.float32)


def split(x):
    high = x.astype(BF16)
    return high, (x - high.astype(F32)).astype(BF16)


def dot3(matrix, x, transposed=False):
    high, low = split(x)
    dims = (((1,), (1 if transposed else 0,)), ((), ()))
    dot = functools.partial(lax.dot_general, dimension_numbers=dims, preferred_element_type=F32)
    return dot(matrix[0], high) + (dot(matrix[0], low) + dot(matrix[1], high))


def two_steps(matrices, k, twist, conj, pair):
    side = 128
    y = dot3(matrices.at[k], jnp.concatenate(pair, axis=1))
    rows = []
    for a in range(2):
        yr, yi = y[:side, a * side:(a + 1) * side], y[side:, a * side:(a + 1) * side]
        if conj:
            tr, ti = yr * twist[0] + yi * twist[1], yi * twist[0] - yr * twist[1]
        else:
            tr, ti = yr * twist[0] - yi * twist[1], yr * twist[1] + yi * twist[0]
        rows.append(jnp.concatenate([tr, ti], axis=1))
    return dot3(matrices.at[k + 1], jnp.concatenate(rows, axis=0), True)


def shrunk(coef, u, limit):
    cr, ci = coef[:128] + u[:128], coef[128:] + u[128:]
    m = jnp.sqrt(cr * cr + ci * ci)
    factor = jnp.maximum(m - limit, 0.0) / jnp.maximum(m, limit)
    return cr * factor, ci * factor


def kernel(
    n_chan, n_tm,
    start_hbm, level_hbm, levels_hbm, coef_hbm, rec_hbm, tables_hbm, twist_hbm, window_hbm,
    coef, rec, last_b, back, twist, limits,
    send_f, recv_f, send_b, recv_b, halo_s, halo_p, send_p, carry, synth, analy, tables, ahead, window,
    start_ref, level_ref, levels_ref,
    in_sem, ssem_f, rsem_f, ssem_b, rsem_b, hsend, hrecv,
):
    me = lax.axis_index("chan")
    t = lax.axis_index("tm")
    before, after = lax.rem(t + n_tm - 1, n_tm), lax.rem(t + 1, n_tm)
    frames = coef.shape[0]
    chunks = frames // CHUNK
    side = 128

    early = [(tables_hbm, tables), (twist_hbm, twist),
             (coef_hbm.at[frames - 1], coef.at[frames - 1]),
             (coef_hbm.at[pl.ds(0, CHUNK - 1)], coef.at[pl.ds(0, CHUNK - 1)])]
    later = [(coef_hbm.at[pl.ds(CHUNK - 1, frames - CHUNK)], coef.at[pl.ds(CHUNK - 1, frames - CHUNK)]),
             (window_hbm, window), (start_hbm, start_ref), (level_hbm, level_ref), (levels_hbm, levels_ref),
             (rec_hbm, rec)]
    loads = [pltpu.make_async_copy(src, dst, in_sem.at[i]) for i, (src, dst) in enumerate(early + later)]

    barrier = pltpu.get_barrier_semaphore()

    def greet(i, _):
        pl.semaphore_signal(barrier, inc=1, device_id={"chan": lax.rem(me + i, n_chan)}, device_id_type=MESH)
        return 0

    lax.fori_loop(1, n_chan, greet, 0)
    for other in (before, after):
        pl.semaphore_signal(barrier, inc=1, device_id={"tm": other}, device_id_type=MESH)
    for load in loads:
        load.start()

    def forward(j):
        for pair in range(CHUNK // 2):
            q = j * CHUNK + 2 * pair
            x = two_steps(ahead, 0, twist, False, [coef[lax.rem(q + a + frames - 1, frames)] for a in range(2)])
            for a in range(2):
                send_f[j, 2 * pair + a] = x[:, a * side:(a + 1) * side]

    def exchange(src, dst, ssem, rsem, j):
        mine = pl.ds(pl.multiple_of(me * 8, 8), 8)

        def send(d):
            pltpu.make_async_remote_copy(
                src_ref=src.at[j, :, pl.ds(pl.multiple_of(d * 8, 8), 8)],
                dst_ref=dst.at[j, :, mine],
                send_sem=ssem.at[j],
                recv_sem=rsem.at[j],
                device_id={"chan": d},
                device_id_type=MESH,
            ).start()

        def both(i, _):
            send(lax.rem(me + i, n_chan))
            send(lax.rem(me + n_chan - i, n_chan))
            return 0

        lax.fori_loop(1, n_chan // 2, both, 0)
        send(lax.rem(me + n_chan // 2, n_chan))
        pltpu.make_async_copy(src.at[j, :, mine], dst.at[j, :, mine], rsem.at[j]).start()

    def wait_bytes(ref, sem):
        pltpu.make_async_copy(ref, ref, sem).wait()

    for load in loads[:len(early)]:
        load.wait()
    for k in range(2):
        ahead[k, 0], ahead[k, 1] = split(tables[k])
    forward(0)
    pl.semaphore_wait(barrier, n_chan + 1)
    exchange(send_f, recv_f, ssem_f, rsem_f, 0)

    def forward_step(j, _):
        forward(j)
        exchange(send_f, recv_f, ssem_f, rsem_f, j)
        return 0

    for load in loads[len(early):-1]:
        load.wait()
    lax.fori_loop(1, chunks, forward_step, 0)

    start = start_ref[0]

    def wave(n_axis, window):
        n_idx = lax.broadcasted_iota(jnp.int32, (side, side), n_axis)
        col = lax.broadcasted_iota(jnp.int32, (side, side), 1 - n_axis)
        later = jnp.where(col < 2 * NB, HOP, 0)
        within = col & (2 * NB - 1)
        phase = ((n_idx + later) * (start + (within >> 1)) + (within & 1) * (FRAME // 4)) & (FRAME - 1)
        return window * jnp.cos(phase.astype(F32) * (2.0 * math.pi / FRAME))

    synth[0], synth[1] = split(2.0 * wave(0, window[0]))
    analy[0], analy[1] = split(wave(1, window[1]))
    carry[...] = jnp.zeros_like(carry)
    limit = levels_ref[level_ref[me]]
    limits[...] = jnp.full(limits.shape, limit, F32)
    for k in range(2):
        back[k, 0], back[k, 1] = split(tables[2 + k])
    loads[-1].wait()

    def spectra(i, tile):
        q = lax.rem(i + 1, frames)
        return recv_f[q // CHUNK, lax.rem(q, CHUNK), pl.ds(tile, 2 * NB, stride=4)]

    def residual_half(i, h, own, following):
        cols = slice(h * 256, (h + 1) * 256)
        est = dot3(synth, jnp.concatenate([jnp.concatenate(own, axis=1), jnp.concatenate(following, axis=1)], axis=0))
        rest = rec[i, :, cols] - est
        rec[i, :, cols] = rest
        return dot3(analy, rest)

    def put(i, tile, value, add=False):
        p = lax.rem(i + frames - 2, frames)
        where = (p // CHUNK, lax.rem(p, CHUNK), pl.ds(tile, 2 * NB, stride=4))
        send_b[where] = value + send_b[where] if add else value

    def step(i, _):
        for h in range(2):
            cols = slice(h * 256, (h + 1) * 256)
            tiles = (2 * h, 2 * h + 1)
            part = residual_half(i, h, [spectra(i, k) for k in tiles], [spectra(i + 1, k) for k in tiles])
            analysed = part[:2 * NB] + carry[:, cols]
            carry[:, cols] = part[2 * NB:]
            for a, k in enumerate(tiles):
                put(i, k, analysed[:, a * side:(a + 1) * side])
        return 0

    wait_bytes(recv_f.at[0], rsem_f.at[0])
    halo_out = pltpu.make_async_remote_copy(
        src_ref=recv_f.at[0, 1], dst_ref=halo_s, send_sem=hsend.at[0], recv_sem=hrecv.at[0],
        device_id={"tm": before}, device_id_type=MESH)
    halo_out.start()
    lax.fori_loop(0, CHUNK - 2, step, 0)

    def middle(j):
        wait_bytes(recv_f.at[j], rsem_f.at[j])
        lax.fori_loop(j * CHUNK - 2, j * CHUNK + 2, step, 0)
        exchange(send_b, recv_b, ssem_b, rsem_b, j - 1)

    middle(1)

    halo_out.wait()
    last = frames - 1
    for h in range(2):
        tiles = (2 * h, 2 * h + 1)
        following = [jnp.where(t < n_tm - 1, halo_s[pl.ds(k, 2 * NB, stride=4)], 0.0) for k in tiles]
        part = residual_half(last, h, [spectra(last, k) for k in tiles], following)
        send_p[:, h * 256:(h + 1) * 256] = part[2 * NB:]
        for a, k in enumerate(tiles):
            put(last, k, part[:2 * NB, a * side:(a + 1) * side])
    part_out = pltpu.make_async_remote_copy(
        src_ref=send_p, dst_ref=halo_p, send_sem=hsend.at[1], recv_sem=hrecv.at[1],
        device_id={"tm": after}, device_id_type=MESH)
    part_out.start()

    def middle_step(j, _):
        middle(j)
        return 0

    lax.fori_loop(2, chunks, middle_step, 0)
    step(frames - 2, 0)
    part_out.wait()
    for k in range(4):
        cols = slice(k * side, (k + 1) * side)
        put(last, k, carry[:, cols], True)
        put(0, k, jnp.where(t > 0, halo_p[:, cols], 0.0), True)
    exchange(send_b, recv_b, ssem_b, rsem_b, chunks - 1)

    def backward(j, _):
        wait_bytes(recv_b.at[j], rsem_b.at[j])
        for pair in range(CHUNK // 2):
            u = two_steps(back, 0, twist, True, [recv_b[j, 2 * pair], recv_b[j, 2 * pair + 1]])
            for a in range(2):
                f = lax.rem(j * CHUNK + 2 * pair + a + 2, frames)
                coef[f, :side], coef[f, side:] = shrunk(coef[f], u[:, a * side:(a + 1) * side], limit)
        return 0

    lax.fori_loop(0, chunks - 1, backward, 0)

    def drain(j, _):
        for buf, sem in ((send_f, ssem_f), (send_b, ssem_b)):
            wait_bytes(buf.at[j, :, pl.ds(0, 8 * (n_chan - 1))], sem.at[j])
        return 0

    lax.fori_loop(0, chunks, drain, 0)
    wait_bytes(recv_b.at[chunks - 1], rsem_b.at[chunks - 1])
    last_b[...] = recv_b[chunks - 1]


def finish(coef, rec, last_b, back, twist, limits, upd_hbm, res_hbm, out, sem):
    frames = coef.shape[0]
    stores = [pltpu.make_async_copy(coef.at[pl.ds(2, frames - CHUNK)], upd_hbm.at[pl.ds(2, frames - CHUNK)], sem.at[0])]
    half = frames // 2
    for i in range(2):
        stores.append(pltpu.make_async_copy(rec.at[pl.ds(i * half, half)], res_hbm.at[pl.ds(i * half, half)], sem.at[1 + i]))
    for store in stores:
        store.start()
    for pair in range(CHUNK // 2):
        u = two_steps(back, 0, twist, True, [last_b[2 * pair], last_b[2 * pair + 1]])
        first = (frames - CHUNK + 2 * pair + 2) % frames
        for a in range(2):
            out[pair, a, :128], out[pair, a, 128:] = shrunk(coef[first + a], u[:, a * 128:(a + 1) * 128], limits[...][:1])
        store = pltpu.make_async_copy(out.at[pair], upd_hbm.at[pl.ds(first, 2)], sem.at[3 + pair])
        store.start()
        stores.append(store)
    for store in stores:
        store.wait()


def body(n_chan, n_tm, record, coefficients, band_start, band_level, levels):
    rows, cols = record.shape
    frames = coefficients.shape[0]
    chunks = frames // CHUNK
    window = window_table()
    tables, twist = dft_tables(n_chan)
    constants = [jnp.asarray(x) for x in (tables, twist, np.stack([window, window.T]))]
    vmem, hbm = (pl.BlockSpec(memory_space=m) for m in (pltpu.VMEM, pltpu.HBM))
    block = pltpu.VMEM((chunks, CHUNK, 8 * n_chan, 128), F32)
    coef_shape = jax.ShapeDtypeStruct((frames, 256, 128), F32)
    rec_shape = jax.ShapeDtypeStruct((frames, HOP, cols), F32)
    parts = pl.pallas_call(
        functools.partial(kernel, n_chan, n_tm),
        out_shape=(
            pltpu.VMEM((frames, 256, 128), F32),
            pltpu.VMEM((frames, HOP, cols), F32),
            pltpu.VMEM((CHUNK, 8 * n_chan, 128), F32),
            pltpu.VMEM((2, 2, 256, 256), BF16),
            pltpu.VMEM((2, 128, 128), F32),
            pltpu.VMEM((8, 128), F32),
        ),
        in_specs=[hbm] * 8,
        out_specs=(vmem,) * 6,
        scratch_shapes=[
            block, block, block, block,
            pltpu.VMEM((8 * n_chan, 128), F32),
            pltpu.VMEM((2 * NB, cols), F32),
            pltpu.VMEM((2 * NB, cols), F32),
            pltpu.VMEM((2 * NB, cols), F32),
            pltpu.VMEM((2, 128, 128), BF16),
            pltpu.VMEM((2, 128, 128), BF16),
            pltpu.VMEM((4, 256, 256), F32),
            pltpu.VMEM((2, 2, 256, 256), BF16),
            pltpu.VMEM((2, 128, 128), F32),
            pltpu.SMEM(band_start.shape, jnp.int32),
            pltpu.SMEM(band_level.shape, jnp.int32),
            pltpu.SMEM(levels.shape, F32),
            pltpu.SemaphoreType.DMA((10,)),
            pltpu.SemaphoreType.DMA((chunks,)),
            pltpu.SemaphoreType.DMA((chunks,)),
            pltpu.SemaphoreType.DMA((chunks,)),
            pltpu.SemaphoreType.DMA((chunks,)),
            pltpu.SemaphoreType.DMA((2,)),
            pltpu.SemaphoreType.DMA((2,)),
        ],
        compiler_params=pltpu.CompilerParams(
            collective_id=0, has_side_effects=True, vmem_limit_bytes=VMEM_LIMIT
        ),
    )(
        band_start, *(pltpu.with_memory_space_constraint(x, pltpu.HBM) for x in (
            band_level, levels,
            coefficients.reshape(frames, 256, 128), record.reshape(frames, HOP, cols), *constants,
        ))
    )
    updated, residual = pl.pallas_call(
        finish,
        out_shape=(coef_shape, rec_shape),
        in_specs=[vmem] * 6,
        out_specs=(hbm, hbm),
        scratch_shapes=[pltpu.VMEM((CHUNK // 2, 2, 256, 128), F32), pltpu.SemaphoreType.DMA((5,))],
        compiler_params=pltpu.CompilerParams(vmem_limit_bytes=VMEM_LIMIT),
    )(*(pltpu.with_memory_space_constraint(x, pltpu.VMEM) for x in parts))
    return updated.reshape(coefficients.shape), residual.reshape(rows, cols)


def solution(mesh):
    return jax.shard_map(
        functools.partial(body, mesh.shape["chan"], mesh.shape["tm"]),
        mesh=mesh,
        in_specs=(P("tm", "chan"), P("tm", None, "chan", None), P(), P(), P()),
        out_specs=(P("tm", None, "chan", None), P("tm", "chan")),
        check_vma=False,
    )
```

```python
import functools
import math

import jax
import jax.numpy as jnp
import numpy as np
from jax import lax
from jax.experimental import pallas as pl
from jax.experimental.pallas import tpu as pltpu
from jax.sharding import PartitionSpec as P

FRAME = 256
HOP = 128
NB = 32
CHUNK = 4
VMEM_LIMIT = 40 * 1024 * 1024
MESH = pl.DeviceIdType.MESH
F32 = jnp.float32
BF16 = jnp.bfloat16


def dft_tables(devices):
    side = 128
    idx = np.arange(side)
    angle = 2.0 * math.pi * (np.outer(idx, idx) % side) / side
    c, s = np.cos(angle), np.sin(angle)
    inverse = np.block([[c, -s], [s, c]])
    per = side // devices
    order = [r * side + d * per + q for d in range(devices) for r in range(2) for q in range(per)]
    second = inverse[order]
    turn = 2.0 * math.pi * np.outer(idx, idx) / side**2
    twist = np.stack([np.cos(turn), np.sin(turn)]).astype(np.float32) / np.float32(side)
    return np.stack([inverse, second, second.T, inverse.T]).astype(np.float32), twist


def window_table():
    n = np.arange(HOP)[:, None] + np.where(np.arange(4 * NB)[None] < 2 * NB, HOP, 0)
    return (np.sin((n + 0.5) * (math.pi / FRAME)) / math.sqrt(FRAME)).astype(np.float32)


def split(x):
    high = x.astype(BF16)
    return high, (x - high.astype(F32)).astype(BF16)


def dot3(matrix, x, transposed=False):
    high, low = split(x)
    dims = (((1,), (1 if transposed else 0,)), ((), ()))
    dot = functools.partial(lax.dot_general, dimension_numbers=dims, preferred_element_type=F32)
    return dot(matrix[0], high) + (dot(matrix[0], low) + dot(matrix[1], high))


def two_steps(matrices, k, twist, conj, pair):
    side = 128
    y = dot3(matrices.at[k], jnp.concatenate(pair, axis=1))
    rows = []
    for a in range(2):
        yr, yi = y[:side, a * side:(a + 1) * side], y[side:, a * side:(a + 1) * side]
        if conj:
            tr, ti = yr * twist[0] + yi * twist[1], yi * twist[0] - yr * twist[1]
        else:
            tr, ti = yr * twist[0] - yi * twist[1], yr * twist[1] + yi * twist[0]
        rows.append(jnp.concatenate([tr, ti], axis=1))
    return dot3(matrices.at[k + 1], jnp.concatenate(rows, axis=0), True)


def shrunk(coef, u, limit):
    cr, ci = coef[:128] + u[:128], coef[128:] + u[128:]
    m = jnp.sqrt(cr * cr + ci * ci)
    factor = jnp.maximum(m - limit, 0.0) / jnp.maximum(m, limit)
    return cr * factor, ci * factor


def kernel(
    n_chan, n_tm,
    start_hbm, level_hbm, levels_hbm, coef_hbm, rec_hbm, tables_hbm, twist_hbm, window_hbm,
    coef, rec, last_b, back, twist, limits,
    send_f, recv_f, send_b, recv_b, halo_s, halo_p, send_p, carry, synth, analy, tables, ahead, window,
    start_ref, level_ref, levels_ref,
    in_sem, ssem_f, rsem_f, ssem_b, rsem_b, hsend, hrecv,
):
    me = lax.axis_index("chan")
    t = lax.axis_index("tm")
    before, after = lax.rem(t + n_tm - 1, n_tm), lax.rem(t + 1, n_tm)
    frames = coef.shape[0]
    chunks = frames // CHUNK
    side = 128

    early = [(tables_hbm, tables), (twist_hbm, twist),
             (coef_hbm.at[frames - 1], coef.at[frames - 1]),
             (coef_hbm.at[pl.ds(0, CHUNK - 1)], coef.at[pl.ds(0, CHUNK - 1)])]
    later = [(coef_hbm.at[pl.ds(CHUNK - 1, frames - CHUNK)], coef.at[pl.ds(CHUNK - 1, frames - CHUNK)]),
             (window_hbm, window), (start_hbm, start_ref), (level_hbm, level_ref), (levels_hbm, levels_ref),
             (rec_hbm, rec)]
    loads = [pltpu.make_async_copy(src, dst, in_sem.at[i]) for i, (src, dst) in enumerate(early + later)]

    barrier = pltpu.get_barrier_semaphore()

    for other in (before, after):
        pl.semaphore_signal(barrier, inc=1, device_id={"tm": other}, device_id_type=MESH)

    def greet(i, _):
        pl.semaphore_signal(barrier, inc=1, device_id={"chan": lax.rem(me + i, n_chan)}, device_id_type=MESH)
        return 0

    lax.fori_loop(1, n_chan, greet, 0)
    for load in loads:
        load.start()

    def forward(j):
        for pair in range(CHUNK // 2):
            q = j * CHUNK + 2 * pair
            x = two_steps(ahead, 0, twist, False, [coef[lax.rem(q + a + frames - 1, frames)] for a in range(2)])
            for a in range(2):
                send_f[j, 2 * pair + a] = x[:, a * side:(a + 1) * side]

    def exchange(src, dst, ssem, rsem, j):
        mine = pl.ds(pl.multiple_of(me * 8, 8), 8)

        def send(d):
            pltpu.make_async_remote_copy(
                src_ref=src.at[j, :, pl.ds(pl.multiple_of(d * 8, 8), 8)],
                dst_ref=dst.at[j, :, mine],
                send_sem=ssem.at[j],
                recv_sem=rsem.at[j],
                device_id={"chan": d},
                device_id_type=MESH,
            ).start()

        def both(i, _):
            send(lax.rem(me + i, n_chan))
            send(lax.rem(me + n_chan - i, n_chan))
            return 0

        lax.fori_loop(1, n_chan // 2, both, 0)
        send(lax.rem(me + n_chan // 2, n_chan))
        pltpu.make_async_copy(src.at[j, :, mine], dst.at[j, :, mine], rsem.at[j]).start()

    def wait_bytes(ref, sem):
        pltpu.make_async_copy(ref, ref, sem).wait()

    for load in loads[:len(early)]:
        load.wait()
    for k in range(2):
        ahead[k, 0], ahead[k, 1] = split(tables[k])
    forward(0)
    pl.semaphore_wait(barrier, n_chan + 1)
    exchange(send_f, recv_f, ssem_f, rsem_f, 0)

    def forward_step(j, _):
        forward(j)
        exchange(send_f, recv_f, ssem_f, rsem_f, j)
        return 0

    for load in loads[len(early):-1]:
        load.wait()
    lax.fori_loop(1, chunks, forward_step, 0)

    start = start_ref[0]

    def wave(n_axis, window):
        n_idx = lax.broadcasted_iota(jnp.int32, (side, side), n_axis)
        col = lax.broadcasted_iota(jnp.int32, (side, side), 1 - n_axis)
        later = jnp.where(col < 2 * NB, HOP, 0)
        within = col & (2 * NB - 1)
        phase = ((n_idx + later) * (start + (within >> 1)) + (within & 1) * (FRAME // 4)) & (FRAME - 1)
        return window * jnp.cos(phase.astype(F32) * (2.0 * math.pi / FRAME))

    synth[0], synth[1] = split(2.0 * wave(0, window[0]))
    analy[0], analy[1] = split(wave(1, window[1]))
    carry[...] = jnp.zeros_like(carry)
    limit = levels_ref[level_ref[me]]
    limits[...] = jnp.full(limits.shape, limit, F32)
    for k in range(2):
        back[k, 0], back[k, 1] = split(tables[2 + k])
    loads[-1].wait()

    def spectra(i, tile):
        q = lax.rem(i + 1, frames)
        return recv_f[q // CHUNK, lax.rem(q, CHUNK), pl.ds(tile, 2 * NB, stride=4)]

    def residual_half(i, h, own, following):
        cols = slice(h * 256, (h + 1) * 256)
        est = dot3(synth, jnp.concatenate([jnp.concatenate(own, axis=1), jnp.concatenate(following, axis=1)], axis=0))
        rest = rec[i, :, cols] - est
        rec[i, :, cols] = rest
        return dot3(analy, rest)

    def put(i, tile, value, add=False):
        p = lax.rem(i + frames - 2, frames)
        where = (p // CHUNK, lax.rem(p, CHUNK), pl.ds(tile, 2 * NB, stride=4))
        send_b[where] = value + send_b[where] if add else value

    def step(i, _):
        for h in range(2):
            cols = slice(h * 256, (h + 1) * 256)
            tiles = (2 * h, 2 * h + 1)
            part = residual_half(i, h, [spectra(i, k) for k in tiles], [spectra(i + 1, k) for k in tiles])
            analysed = part[:2 * NB] + carry[:, cols]
            carry[:, cols] = part[2 * NB:]
            for a, k in enumerate(tiles):
                put(i, k, analysed[:, a * side:(a + 1) * side])
        return 0

    wait_bytes(recv_f.at[0], rsem_f.at[0])
    halo_out = pltpu.make_async_remote_copy(
        src_ref=recv_f.at[0, 1], dst_ref=halo_s, send_sem=hsend.at[0], recv_sem=hrecv.at[0],
        device_id={"tm": before}, device_id_type=MESH)
    halo_out.start()
    lax.fori_loop(0, CHUNK - 2, step, 0)

    def middle(j):
        wait_bytes(recv_f.at[j], rsem_f.at[j])
        lax.fori_loop(j * CHUNK - 2, j * CHUNK + 2, step, 0)
        exchange(send_b, recv_b, ssem_b, rsem_b, j - 1)

    middle(1)

    halo_out.wait()
    last = frames - 1
    for h in range(2):
        tiles = (2 * h, 2 * h + 1)
        following = [jnp.where(t < n_tm - 1, halo_s[pl.ds(k, 2 * NB, stride=4)], 0.0) for k in tiles]
        part = residual_half(last, h, [spectra(last, k) for k in tiles], following)
        send_p[:, h * 256:(h + 1) * 256] = part[2 * NB:]
        for a, k in enumerate(tiles):
            put(last, k, part[:2 * NB, a * side:(a + 1) * side])
    part_out = pltpu.make_async_remote_copy(
        src_ref=send_p, dst_ref=halo_p, send_sem=hsend.at[1], recv_sem=hrecv.at[1],
        device_id={"tm": after}, device_id_type=MESH)
    part_out.start()

    def middle_step(j, _):
        middle(j)
        return 0

    lax.fori_loop(2, chunks, middle_step, 0)
    step(frames - 2, 0)
    part_out.wait()
    for k in range(4):
        cols = slice(k * side, (k + 1) * side)
        put(last, k, carry[:, cols], True)
        put(0, k, jnp.where(t > 0, halo_p[:, cols], 0.0), True)
    exchange(send_b, recv_b, ssem_b, rsem_b, chunks - 1)

    def backward(j, _):
        wait_bytes(recv_b.at[j], rsem_b.at[j])
        for pair in range(CHUNK // 2):
            u = two_steps(back, 0, twist, True, [recv_b[j, 2 * pair], recv_b[j, 2 * pair + 1]])
            for a in range(2):
                f = lax.rem(j * CHUNK + 2 * pair + a + 2, frames)
                coef[f, :side], coef[f, side:] = shrunk(coef[f], u[:, a * side:(a + 1) * side], limit)
        return 0

    lax.fori_loop(0, chunks - 1, backward, 0)

    def drain(j, _):
        for buf, sem in ((send_f, ssem_f), (send_b, ssem_b)):
            wait_bytes(buf.at[j, :, pl.ds(0, 8 * (n_chan - 1))], sem.at[j])
        return 0

    lax.fori_loop(0, chunks, drain, 0)
    wait_bytes(recv_b.at[chunks - 1], rsem_b.at[chunks - 1])
    last_b[...] = recv_b[chunks - 1]


def finish(coef, rec, last_b, back, twist, limits, upd_hbm, res_hbm, out, sem):
    frames = coef.shape[0]
    stores = [pltpu.make_async_copy(coef.at[pl.ds(2, frames - CHUNK)], upd_hbm.at[pl.ds(2, frames - CHUNK)], sem.at[0])]
    half = frames // 2
    for i in range(2):
        stores.append(pltpu.make_async_copy(rec.at[pl.ds(i * half, half)], res_hbm.at[pl.ds(i * half, half)], sem.at[1 + i]))
    for store in stores:
        store.start()
    for pair in range(CHUNK // 2):
        u = two_steps(back, 0, twist, True, [last_b[2 * pair], last_b[2 * pair + 1]])
        first = (frames - CHUNK + 2 * pair + 2) % frames
        for a in range(2):
            out[pair, a, :128], out[pair, a, 128:] = shrunk(coef[first + a], u[:, a * 128:(a + 1) * 128], limits[...][:1])
        store = pltpu.make_async_copy(out.at[pair], upd_hbm.at[pl.ds(first, 2)], sem.at[3 + pair])
        store.start()
        stores.append(store)
    for store in stores:
        store.wait()


def body(n_chan, n_tm, record, coefficients, band_start, band_level, levels):
    rows, cols = record.shape
    frames = coefficients.shape[0]
    chunks = frames // CHUNK
    window = window_table()
    tables, twist = dft_tables(n_chan)
    constants = [jnp.asarray(x) for x in (tables, twist, np.stack([window, window.T]))]
    vmem, hbm = (pl.BlockSpec(memory_space=m) for m in (pltpu.VMEM, pltpu.HBM))
    block = pltpu.VMEM((chunks, CHUNK, 8 * n_chan, 128), F32)
    coef_shape = jax.ShapeDtypeStruct((frames, 256, 128), F32)
    rec_shape = jax.ShapeDtypeStruct((frames, HOP, cols), F32)
    parts = pl.pallas_call(
        functools.partial(kernel, n_chan, n_tm),
        out_shape=(
            pltpu.VMEM((frames, 256, 128), F32),
            pltpu.VMEM((frames, HOP, cols), F32),
            pltpu.VMEM((CHUNK, 8 * n_chan, 128), F32),
            pltpu.VMEM((2, 2, 256, 256), BF16),
            pltpu.VMEM((2, 128, 128), F32),
            pltpu.VMEM((8, 128), F32),
        ),
        in_specs=[hbm] * 8,
        out_specs=(vmem,) * 6,
        scratch_shapes=[
            block, block, block, block,
            pltpu.VMEM((8 * n_chan, 128), F32),
            pltpu.VMEM((2 * NB, cols), F32),
            pltpu.VMEM((2 * NB, cols), F32),
            pltpu.VMEM((2 * NB, cols), F32),
            pltpu.VMEM((2, 128, 128), BF16),
            pltpu.VMEM((2, 128, 128), BF16),
            pltpu.VMEM((4, 256, 256), F32),
            pltpu.VMEM((2, 2, 256, 256), BF16),
            pltpu.VMEM((2, 128, 128), F32),
            pltpu.SMEM(band_start.shape, jnp.int32),
            pltpu.SMEM(band_level.shape, jnp.int32),
            pltpu.SMEM(levels.shape, F32),
            pltpu.SemaphoreType.DMA((10,)),
            pltpu.SemaphoreType.DMA((chunks,)),
            pltpu.SemaphoreType.DMA((chunks,)),
            pltpu.SemaphoreType.DMA((chunks,)),
            pltpu.SemaphoreType.DMA((chunks,)),
            pltpu.SemaphoreType.DMA((2,)),
            pltpu.SemaphoreType.DMA((2,)),
        ],
        compiler_params=pltpu.CompilerParams(
            collective_id=0, has_side_effects=True, vmem_limit_bytes=VMEM_LIMIT
        ),
    )(
        band_start, *(pltpu.with_memory_space_constraint(x, pltpu.HBM) for x in (
            band_level, levels,
            coefficients.reshape(frames, 256, 128), record.reshape(frames, HOP, cols), *constants,
        ))
    )
    updated, residual = pl.pallas_call(
        finish,
        out_shape=(coef_shape, rec_shape),
        in_specs=[vmem] * 6,
        out_specs=(hbm, hbm),
        scratch_shapes=[pltpu.VMEM((CHUNK // 2, 2, 256, 128), F32), pltpu.SemaphoreType.DMA((5,))],
        compiler_params=pltpu.CompilerParams(vmem_limit_bytes=VMEM_LIMIT),
    )(*(pltpu.with_memory_space_constraint(x, pltpu.VMEM) for x in parts))
    return updated.reshape(coefficients.shape), residual.reshape(rows, cols)


def solution(mesh):
    return jax.shard_map(
        functools.partial(body, mesh.shape["chan"], mesh.shape["tm"]),
        mesh=mesh,
        in_specs=(P("tm", "chan"), P("tm", None, "chan", None), P(), P(), P()),
        out_specs=(P("tm", None, "chan", None), P("tm", "chan")),
        check_vma=False,
    )
```

```python
import functools
import math

import jax
import jax.numpy as jnp
import numpy as np
from jax import lax
from jax.experimental import pallas as pl
from jax.experimental.pallas import tpu as pltpu
from jax.sharding import PartitionSpec as P

FRAME = 256
HOP = 128
NB = 32
CHUNK = 4
VMEM_LIMIT = 40 * 1024 * 1024
MESH = pl.DeviceIdType.MESH
F32 = jnp.float32
BF16 = jnp.bfloat16


def dft_tables(devices):
    side = 128
    idx = np.arange(side)
    angle = 2.0 * math.pi * (np.outer(idx, idx) % side) / side
    c, s = np.cos(angle), np.sin(angle)
    inverse = np.block([[c, -s], [s, c]])
    per = side // devices
    order = [r * side + d * per + q for d in range(devices) for r in range(2) for q in range(per)]
    second = inverse[order]
    turn = 2.0 * math.pi * np.outer(idx, idx) / side**2
    twist = np.stack([np.cos(turn), np.sin(turn)]).astype(np.float32) / np.float32(side)
    return np.stack([inverse, second, second.T, inverse.T]).astype(np.float32), twist


def window_table():
    n = np.arange(HOP)[:, None] + np.where(np.arange(4 * NB)[None] < 2 * NB, HOP, 0)
    return (np.sin((n + 0.5) * (math.pi / FRAME)) / math.sqrt(FRAME)).astype(np.float32)


def split(x):
    high = x.astype(BF16)
    return high, (x - high.astype(F32)).astype(BF16)


def dot3(matrix, x, transposed=False):
    high, low = split(x)
    dims = (((1,), (1 if transposed else 0,)), ((), ()))
    dot = functools.partial(lax.dot_general, dimension_numbers=dims, preferred_element_type=F32)
    return dot(matrix[0], high) + (dot(matrix[0], low) + dot(matrix[1], high))


def two_steps(matrices, k, twist, conj, pair):
    side = 128
    y = dot3(matrices.at[k], jnp.concatenate(pair, axis=1))
    rows = []
    for a in range(2):
        yr, yi = y[:side, a * side:(a + 1) * side], y[side:, a * side:(a + 1) * side]
        if conj:
            tr, ti = yr * twist[0] + yi * twist[1], yi * twist[0] - yr * twist[1]
        else:
            tr, ti = yr * twist[0] - yi * twist[1], yr * twist[1] + yi * twist[0]
        rows.append(jnp.concatenate([tr, ti], axis=1))
    return dot3(matrices.at[k + 1], jnp.concatenate(rows, axis=0), True)


def shrunk(coef, u, limit):
    cr, ci = coef[:128] + u[:128], coef[128:] + u[128:]
    m = jnp.sqrt(cr * cr + ci * ci)
    factor = jnp.maximum(m - limit, 0.0) / jnp.maximum(m, limit)
    return cr * factor, ci * factor


def kernel(
    n_chan, n_tm,
    start_hbm, level_hbm, levels_hbm, coef_hbm, rec_hbm, tables_hbm, twist_hbm, window_hbm,
    coef, rec, last_b, back, twist, limits,
    send_f, recv_f, send_b, recv_b, halo_s, halo_p, send_p, carry, synth, analy, tables, ahead, window,
    start_ref, level_ref, levels_ref,
    in_sem, ssem_f, rsem_f, ssem_b, rsem_b, hsend, hrecv,
):
    me = lax.axis_index("chan")
    t = lax.axis_index("tm")
    before, after = lax.rem(t + n_tm - 1, n_tm), lax.rem(t + 1, n_tm)
    frames = coef.shape[0]
    chunks = frames // CHUNK
    side = 128

    early = [(tables_hbm, tables), (twist_hbm, twist),
             (coef_hbm.at[frames - 1], coef.at[frames - 1]),
             (coef_hbm.at[pl.ds(0, CHUNK - 1)], coef.at[pl.ds(0, CHUNK - 1)])]
    later = [(coef_hbm.at[pl.ds(CHUNK - 1, frames - CHUNK)], coef.at[pl.ds(CHUNK - 1, frames - CHUNK)]),
             (window_hbm, window), (start_hbm, start_ref), (level_hbm, level_ref), (levels_hbm, levels_ref),
             (rec_hbm, rec)]
    loads = [pltpu.make_async_copy(src, dst, in_sem.at[i]) for i, (src, dst) in enumerate(early + later)]

    barrier = pltpu.get_barrier_semaphore()

    for other in (before, after):
        pl.semaphore_signal(barrier, inc=1, device_id={"tm": other}, device_id_type=MESH)

    def greet(offset):
        pl.semaphore_signal(barrier, inc=1, device_id={"chan": lax.rem(me + offset, n_chan)}, device_id_type=MESH)

    def greet_both(i, _):
        greet(n_chan // 2 - i)
        greet(n_chan // 2 + i)
        return 0

    greet(n_chan // 2)
    lax.fori_loop(1, n_chan // 2, greet_both, 0)
    for load in loads:
        load.start()

    def forward(j):
        for pair in range(CHUNK // 2):
            q = j * CHUNK + 2 * pair
            x = two_steps(ahead, 0, twist, False, [coef[lax.rem(q + a + frames - 1, frames)] for a in range(2)])
            for a in range(2):
                send_f[j, 2 * pair + a] = x[:, a * side:(a + 1) * side]

    def exchange(src, dst, ssem, rsem, j):
        mine = pl.ds(pl.multiple_of(me * 8, 8), 8)

        def send(d):
            pltpu.make_async_remote_copy(
                src_ref=src.at[j, :, pl.ds(pl.multiple_of(d * 8, 8), 8)],
                dst_ref=dst.at[j, :, mine],
                send_sem=ssem.at[j],
                recv_sem=rsem.at[j],
                device_id={"chan": d},
                device_id_type=MESH,
            ).start()

        def both(i, _):
            send(lax.rem(me + i, n_chan))
            send(lax.rem(me + n_chan - i, n_chan))
            return 0

        lax.fori_loop(1, n_chan // 2, both, 0)
        send(lax.rem(me + n_chan // 2, n_chan))
        pltpu.make_async_copy(src.at[j, :, mine], dst.at[j, :, mine], rsem.at[j]).start()

    def wait_bytes(ref, sem):
        pltpu.make_async_copy(ref, ref, sem).wait()

    for load in loads[:len(early)]:
        load.wait()
    for k in range(2):
        ahead[k, 0], ahead[k, 1] = split(tables[k])
    forward(0)
    pl.semaphore_wait(barrier, n_chan + 1)
    exchange(send_f, recv_f, ssem_f, rsem_f, 0)

    def forward_step(j, _):
        forward(j)
        exchange(send_f, recv_f, ssem_f, rsem_f, j)
        return 0

    for load in loads[len(early):-1]:
        load.wait()
    lax.fori_loop(1, chunks, forward_step, 0)

    start = start_ref[0]

    def wave(n_axis, window):
        n_idx = lax.broadcasted_iota(jnp.int32, (side, side), n_axis)
        col = lax.broadcasted_iota(jnp.int32, (side, side), 1 - n_axis)
        later = jnp.where(col < 2 * NB, HOP, 0)
        within = col & (2 * NB - 1)
        phase = ((n_idx + later) * (start + (within >> 1)) + (within & 1) * (FRAME // 4)) & (FRAME - 1)
        return window * jnp.cos(phase.astype(F32) * (2.0 * math.pi / FRAME))

    synth[0], synth[1] = split(2.0 * wave(0, window[0]))
    analy[0], analy[1] = split(wave(1, window[1]))
    carry[...] = jnp.zeros_like(carry)
    limit = levels_ref[level_ref[me]]
    limits[...] = jnp.full(limits.shape, limit, F32)
    for k in range(2):
        back[k, 0], back[k, 1] = split(tables[2 + k])
    loads[-1].wait()

    def spectra(i, tile):
        q = lax.rem(i + 1, frames)
        return recv_f[q // CHUNK, lax.rem(q, CHUNK), pl.ds(tile, 2 * NB, stride=4)]

    def residual_half(i, h, own, following):
        cols = slice(h * 256, (h + 1) * 256)
        est = dot3(synth, jnp.concatenate([jnp.concatenate(own, axis=1), jnp.concatenate(following, axis=1)], axis=0))
        rest = rec[i, :, cols] - est
        rec[i, :, cols] = rest
        return dot3(analy, rest)

    def put(i, tile, value, add=False):
        p = lax.rem(i + frames - 2, frames)
        where = (p // CHUNK, lax.rem(p, CHUNK), pl.ds(tile, 2 * NB, stride=4))
        send_b[where] = value + send_b[where] if add else value

    def step(i, _):
        for h in range(2):
            cols = slice(h * 256, (h + 1) * 256)
            tiles = (2 * h, 2 * h + 1)
            part = residual_half(i, h, [spectra(i, k) for k in tiles], [spectra(i + 1, k) for k in tiles])
            analysed = part[:2 * NB] + carry[:, cols]
            carry[:, cols] = part[2 * NB:]
            for a, k in enumerate(tiles):
                put(i, k, analysed[:, a * side:(a + 1) * side])
        return 0

    wait_bytes(recv_f.at[0], rsem_f.at[0])
    halo_out = pltpu.make_async_remote_copy(
        src_ref=recv_f.at[0, 1], dst_ref=halo_s, send_sem=hsend.at[0], recv_sem=hrecv.at[0],
        device_id={"tm": before}, device_id_type=MESH)
    halo_out.start()
    lax.fori_loop(0, CHUNK - 2, step, 0)

    def middle(j):
        wait_bytes(recv_f.at[j], rsem_f.at[j])
        lax.fori_loop(j * CHUNK - 2, j * CHUNK + 2, step, 0)
        exchange(send_b, recv_b, ssem_b, rsem_b, j - 1)

    middle(1)

    halo_out.wait()
    last = frames - 1
    for h in range(2):
        tiles = (2 * h, 2 * h + 1)
        following = [jnp.where(t < n_tm - 1, halo_s[pl.ds(k, 2 * NB, stride=4)], 0.0) for k in tiles]
        part = residual_half(last, h, [spectra(last, k) for k in tiles], following)
        send_p[:, h * 256:(h + 1) * 256] = part[2 * NB:]
        for a, k in enumerate(tiles):
            put(last, k, part[:2 * NB, a * side:(a + 1) * side])
    part_out = pltpu.make_async_remote_copy(
        src_ref=send_p, dst_ref=halo_p, send_sem=hsend.at[1], recv_sem=hrecv.at[1],
        device_id={"tm": after}, device_id_type=MESH)
    part_out.start()

    def middle_step(j, _):
        middle(j)
        return 0

    lax.fori_loop(2, chunks, middle_step, 0)
    step(frames - 2, 0)
    part_out.wait()
    for k in range(4):
        cols = slice(k * side, (k + 1) * side)
        put(last, k, carry[:, cols], True)
        put(0, k, jnp.where(t > 0, halo_p[:, cols], 0.0), True)
    exchange(send_b, recv_b, ssem_b, rsem_b, chunks - 1)

    def backward(j, _):
        wait_bytes(recv_b.at[j], rsem_b.at[j])
        for pair in range(CHUNK // 2):
            u = two_steps(back, 0, twist, True, [recv_b[j, 2 * pair], recv_b[j, 2 * pair + 1]])
            for a in range(2):
                f = lax.rem(j * CHUNK + 2 * pair + a + 2, frames)
                coef[f, :side], coef[f, side:] = shrunk(coef[f], u[:, a * side:(a + 1) * side], limit)
        return 0

    lax.fori_loop(0, chunks - 1, backward, 0)

    def drain(j, _):
        for buf, sem in ((send_f, ssem_f), (send_b, ssem_b)):
            wait_bytes(buf.at[j, :, pl.ds(0, 8 * (n_chan - 1))], sem.at[j])
        return 0

    lax.fori_loop(0, chunks, drain, 0)
    wait_bytes(recv_b.at[chunks - 1], rsem_b.at[chunks - 1])
    last_b[...] = recv_b[chunks - 1]


def finish(coef, rec, last_b, back, twist, limits, upd_hbm, res_hbm, out, sem):
    frames = coef.shape[0]
    stores = [pltpu.make_async_copy(coef.at[pl.ds(2, frames - CHUNK)], upd_hbm.at[pl.ds(2, frames - CHUNK)], sem.at[0])]
    half = frames // 2
    for i in range(2):
        stores.append(pltpu.make_async_copy(rec.at[pl.ds(i * half, half)], res_hbm.at[pl.ds(i * half, half)], sem.at[1 + i]))
    for store in stores:
        store.start()
    for pair in range(CHUNK // 2):
        u = two_steps(back, 0, twist, True, [last_b[2 * pair], last_b[2 * pair + 1]])
        first = (frames - CHUNK + 2 * pair + 2) % frames
        for a in range(2):
            out[pair, a, :128], out[pair, a, 128:] = shrunk(coef[first + a], u[:, a * 128:(a + 1) * 128], limits[...][:1])
        store = pltpu.make_async_copy(out.at[pair], upd_hbm.at[pl.ds(first, 2)], sem.at[3 + pair])
        store.start()
        stores.append(store)
    for store in stores:
        store.wait()


def body(n_chan, n_tm, record, coefficients, band_start, band_level, levels):
    rows, cols = record.shape
    frames = coefficients.shape[0]
    chunks = frames // CHUNK
    window = window_table()
    tables, twist = dft_tables(n_chan)
    constants = [jnp.asarray(x) for x in (tables, twist, np.stack([window, window.T]))]
    vmem, hbm = (pl.BlockSpec(memory_space=m) for m in (pltpu.VMEM, pltpu.HBM))
    block = pltpu.VMEM((chunks, CHUNK, 8 * n_chan, 128), F32)
    coef_shape = jax.ShapeDtypeStruct((frames, 256, 128), F32)
    rec_shape = jax.ShapeDtypeStruct((frames, HOP, cols), F32)
    parts = pl.pallas_call(
        functools.partial(kernel, n_chan, n_tm),
        out_shape=(
            pltpu.VMEM((frames, 256, 128), F32),
            pltpu.VMEM((frames, HOP, cols), F32),
            pltpu.VMEM((CHUNK, 8 * n_chan, 128), F32),
            pltpu.VMEM((2, 2, 256, 256), BF16),
            pltpu.VMEM((2, 128, 128), F32),
            pltpu.VMEM((8, 128), F32),
        ),
        in_specs=[hbm] * 8,
        out_specs=(vmem,) * 6,
        scratch_shapes=[
            block, block, block, block,
            pltpu.VMEM((8 * n_chan, 128), F32),
            pltpu.VMEM((2 * NB, cols), F32),
            pltpu.VMEM((2 * NB, cols), F32),
            pltpu.VMEM((2 * NB, cols), F32),
            pltpu.VMEM((2, 128, 128), BF16),
            pltpu.VMEM((2, 128, 128), BF16),
            pltpu.VMEM((4, 256, 256), F32),
            pltpu.VMEM((2, 2, 256, 256), BF16),
            pltpu.VMEM((2, 128, 128), F32),
            pltpu.SMEM(band_start.shape, jnp.int32),
            pltpu.SMEM(band_level.shape, jnp.int32),
            pltpu.SMEM(levels.shape, F32),
            pltpu.SemaphoreType.DMA((10,)),
            pltpu.SemaphoreType.DMA((chunks,)),
            pltpu.SemaphoreType.DMA((chunks,)),
            pltpu.SemaphoreType.DMA((chunks,)),
            pltpu.SemaphoreType.DMA((chunks,)),
            pltpu.SemaphoreType.DMA((2,)),
            pltpu.SemaphoreType.DMA((2,)),
        ],
        compiler_params=pltpu.CompilerParams(
            collective_id=0, has_side_effects=True, vmem_limit_bytes=VMEM_LIMIT
        ),
    )(
        band_start, *(pltpu.with_memory_space_constraint(x, pltpu.HBM) for x in (
            band_level, levels,
            coefficients.reshape(frames, 256, 128), record.reshape(frames, HOP, cols), *constants,
        ))
    )
    updated, residual = pl.pallas_call(
        finish,
        out_shape=(coef_shape, rec_shape),
        in_specs=[vmem] * 6,
        out_specs=(hbm, hbm),
        scratch_shapes=[pltpu.VMEM((CHUNK // 2, 2, 256, 128), F32), pltpu.SemaphoreType.DMA((5,))],
        compiler_params=pltpu.CompilerParams(vmem_limit_bytes=VMEM_LIMIT),
    )(*(pltpu.with_memory_space_constraint(x, pltpu.VMEM) for x in parts))
    return updated.reshape(coefficients.shape), residual.reshape(rows, cols)


def solution(mesh):
    return jax.shard_map(
        functools.partial(body, mesh.shape["chan"], mesh.shape["tm"]),
        mesh=mesh,
        in_specs=(P("tm", "chan"), P("tm", None, "chan", None), P(), P(), P()),
        out_specs=(P("tm", None, "chan", None), P("tm", "chan")),
        check_vma=False,
    )
```
